512 devices in a mesh: dp: 32 (over z, core), mp: 16 (over y, x).
Axes of the slice: x: 4, y: 4, z: 16, core: 2. Of those that a mesh axis runs over, the one named last changes fastest.
Arguments:
- hidden_codes: int32 [6144, 3584], P('dp', 'mp'), parts along dimension 0, may hold values from -32768 to 32767, as said below
- token_scales: float32 [6144], P('dp'), parts along dimension 0, may hold values from 0.08 to 0.4
- weight_codes: int32 [14336, 1024], P('mp'), may hold values from -32768 to 32767, as said below
- column_scales: float32 [4096], P('mp'), may hold values from 0.0008 to 0.004
Outputs:
- layer_output: bfloat16 [6144, 4096], P('dp', 'mp'), parts along dimension 0
The draws below stay inside these ranges and needn't reach their ends.
There are 32 independent parts, one for each index of `dp`. The reference program is written for one: setup_inputs(seed, part) draws one part's arguments, and reference() takes and returns one part's arrays. A program takes and returns all parts, laid end to end along the dimension named above; an argument that names none is the same for every part. Nothing has to cross between parts.
Inputs may be any that keep to these rules, and one draw needn't show every extreme that they name: `hidden_codes`: each word is u0 + 16 u1 + 256 u2 + 4096 s3 with u0, u1, u2 in 0..15 and s3 in -8..7. `weight_codes`: each word is u0 + 16 u1 + 256 u2 + 4096 s3 with u0, u1, u2 in 0..15 and s3 in -8..7.
All inputs are finite; a program needn't handle non-finite values.
Results may differ from the reference program's by a relative error of at most 0.025.
Values may be sent and summed in bfloat16 or wider, within the bound.
A program may use at most 64 MiB of HBM per device.

```python
import math
import jax
import jax.numpy as jnp
import numpy as np
from jax import lax

D = 4096
HC = 28
TOKENS = 192
HB = 512
FF = 14336
N_MP = 16


def pack_words(key, row_count, word_count):
    nibble_keys = jax.random.split(key, 4)
    lower = [jax.random.randint(nibble_keys[position], (row_count, word_count), 0, 16, dtype=jnp.int32) for position in range(3)]
    highest = jax.random.randint(nibble_keys[3], (row_count, word_count), -8, 8, dtype=jnp.int32)
    return lower[0] + 16 * lower[1] + 256 * lower[2] + 4096 * highest


def draw_hidden_codes(key, part):
    key = jax.random.fold_in(key, 11)
    return pack_words(key, TOKENS, FF // 4)


def draw_weight_codes(key, part):
    key = jax.random.fold_in(key, 12)
    return pack_words(key, FF, D // 4)


def levels(rng, shape, cuts, low, high):
    def one(dim, blocks):
        steps = jax.random.uniform(jax.random.fold_in(jax.random.fold_in(rng, 6), dim), (blocks,), jnp.float32, low / len(cuts), high / len(cuts))
        return jnp.repeat(jnp.exp(steps), shape[dim] // blocks).reshape((-1,) + (1,) * (len(shape) - dim - 1))

    loudness = one(*cuts[0])
    for cut in cuts[1:]:
        loudness = loudness * one(*cut)
    return loudness


def setup_inputs(seed: int = 0, part: int = 0) -> dict:
    streams_of = jax.random.split(jax.random.key(seed), 5)
    own_keys = jax.random.split(jax.random.fold_in(streams_of[4], part), 5)
    hidden_codes = draw_hidden_codes(jax.random.fold_in(jax.random.fold_in(streams_of[4], part), 71), part)
    token_scales = jnp.clip(jnp.exp(jax.random.uniform(own_keys[1], (TOKENS,), jnp.float32, math.log(0.08), math.log(0.4))), 0.08, 0.4)
    weight_codes = draw_weight_codes(jax.random.fold_in(streams_of[4], 71), part)
    column_scales = jnp.clip(jnp.exp(math.log(0.004) - 1.609438 * jax.random.uniform(streams_of[3], (D,), jnp.float32) ** levels(streams_of[3], (D,), ((0, 16),), -0.2, 0.2)), 0.0008, 0.004)
    return {"hidden_codes": hidden_codes, "token_scales": token_scales, "weight_codes": weight_codes, "column_scales": column_scales}


def paley_table():
    modulus = 13
    residues = set((value * value % modulus for value in range(1, modulus)))
    symbols = np.array([0.0] + [1.0 if value in residues else -1.0 for value in range(1, modulus)])
    indices = np.arange(modulus)
    jacobsthal = symbols[(indices[None, :] - indices[:, None]) % modulus]
    first_row = np.concatenate([np.zeros((1, 1)), np.ones((1, modulus))], axis=1)
    other_rows = np.concatenate([np.ones((modulus, 1)), jacobsthal], axis=1)
    conference = np.concatenate([first_row, other_rows], axis=0)
    return np.kron(conference, np.array([[1.0, 1.0], [1.0, -1.0]])) + np.kron(np.eye(modulus + 1), np.array([[1.0, -1.0], [-1.0, -1.0]]))

def sylvester_table(length):
    indices = np.arange(length)
    intersection = indices[:, None] & indices[None, :]
    parity = intersection & 1
    for shift in range(1, max(length, 2).bit_length()):
        parity = parity ^ intersection >> shift & 1
    return 1.0 - 2.0 * parity

def unpack_words(packed):
    return [packed % 16 - 8, packed // 16 % 16 - 8, packed // 256 % 16 - 8, packed // 4096]

def reference(hidden_codes, token_scales, weight_codes, column_scales):
    codes = jnp.stack(unpack_words(hidden_codes), axis=2).reshape(TOKENS, FF)
    hidden = lax.optimization_barrier((codes.astype(jnp.float32) * token_scales[:, None]).astype(jnp.bfloat16))
    blocks = hidden.astype(jnp.float32).reshape(TOKENS, HB, HC)
    paley = jnp.asarray(paley_table(), jnp.float32)
    sylvester = jnp.asarray(sylvester_table(HB), jnp.float32)
    mixed = jnp.einsum('tba,ae->tbe', blocks, paley, precision=lax.Precision.HIGHEST)
    mixed = jnp.einsum('tba,bc->tca', mixed, sylvester, precision=lax.Precision.HIGHEST)
    rotated = (mixed.reshape(TOKENS, FF) * (1.0 / math.sqrt(FF))).astype(jnp.bfloat16)
    block_rows = FF // N_MP
    summed = jnp.zeros((TOKENS, D), jnp.float32)
    for block in range(N_MP):
        packed = weight_codes[block * block_rows:(block + 1) * block_rows]
        weights = jnp.concatenate(unpack_words(packed), axis=1).astype(jnp.bfloat16)
        partial_term = jnp.dot(rotated[:, block * block_rows:(block + 1) * block_rows], weights, preferred_element_type=jnp.float32)
        rounded = lax.optimization_barrier(partial_term.astype(jnp.bfloat16))
        summed = summed + rounded.astype(jnp.float32)
    return (summed * column_scales[None, :]).astype(jnp.bfloat16)
```

```python
import math

import jax
import jax.numpy as jnp
import numpy as np
from jax import lax
from jax.experimental import pallas as pl
from jax.experimental.pallas import tpu as pltpu
from jax.sharding import PartitionSpec as P

HC = 28
FF = 14336
SIDE = 4
N_MP = 16
T = 192
WORDS = 224
WIDE = 256
UNITS = 896
SLICE = 48
HALF = 128
F32 = jnp.float32
BF16 = jnp.bfloat16
MESH = pl.DeviceIdType.MESH

OFFSETS = sorted(
    [(dy, dx) for dy in range(SIDE) for dx in range(SIDE)],
    key=lambda o: -(min(o[0], SIDE - o[0]) + min(o[1], SIDE - o[1])),
)
PEERS = [o for o in OFFSETS if o != (0, 0)]
ORDER = [
    (2, 2), (2, 1), (2, 3), (1, 2), (3, 2), (2, 0), (0, 2), (1, 1),
    (1, 3), (3, 1), (3, 3), (1, 0), (0, 1), (3, 0), (0, 3), (0, 0),
]


def paley_table():
    modulus = 13
    residues = set((value * value % modulus for value in range(1, modulus)))
    symbols = np.array([0.0] + [1.0 if value in residues else -1.0 for value in range(1, modulus)])
    indices = np.arange(modulus)
    jacobsthal = symbols[(indices[None, :] - indices[:, None]) % modulus]
    first_row = np.concatenate([np.zeros((1, 1)), np.ones((1, modulus))], axis=1)
    other_rows = np.concatenate([np.ones((modulus, 1)), jacobsthal], axis=1)
    conference = np.concatenate([first_row, other_rows], axis=0)
    return np.kron(conference, np.array([[1.0, 1.0], [1.0, -1.0]])) + np.kron(
        np.eye(modulus + 1), np.array([[1.0, -1.0], [-1.0, -1.0]])
    )


def sylvester_table(length):
    indices = np.arange(length)
    intersection = indices[:, None] & indices[None, :]
    parity = intersection & 1
    for shift in range(1, max(length, 2).bit_length()):
        parity = parity ^ intersection >> shift & 1
    return 1.0 - 2.0 * parity


def local_table():
    table = np.kron(sylvester_table(UNITS // HC), paley_table())
    rows = 4 * np.arange(WORDS)[None, :] + np.arange(4)[:, None]
    out = np.zeros((4, WIDE, UNITS), np.float32)
    out[:, :WORDS] = table[rows]
    return out


def nibble(flipped, k):
    if k == 3:
        return flipped >> 12
    return (flipped << (28 - 4 * k)) >> 28


def hadamard(values):
    step = 1
    while step < len(values):
        values = [
            values[i ^ step] - values[i] if i & step else values[i] + values[i ^ step]
            for i in range(len(values))
        ]
        step *= 2
    return values


def kernel(
    hc_hbm, ts_hbm, w_hbm, cs_hbm, r_hbm, out_ref,
    hc, ts_ref, w, cs_ref, r, codes, gathered, mixed, z, rot, wbf, ts_col,
    sa, sb, ra, rb, ta, tb, fa, fb,
    hc_sem, ts_sem, w_sem, cs_sem, r_sem, g_send, g_recv, z_send, z_recv,
    a_send, a_recv, b_send, b_recv, ta_send, ta_recv, tb_send, tb_recv,
):
    me = lax.axis_index("mp")
    y, x = me // SIDE, me % SIDE

    def at(dy, dx):
        return lax.rem(y + dy, SIDE) * SIDE + lax.rem(x + dx, SIDE)

    def remote(src, dst, send, recv, target):
        return pltpu.make_async_remote_copy(
            src_ref=src, dst_ref=dst, send_sem=send, recv_sem=recv,
            device_id={"mp": target}, device_id_type=MESH,
        )

    barrier = pltpu.get_barrier_semaphore()
    for offset in PEERS:
        pl.semaphore_signal(barrier, inc=1, device_id={"mp": at(*offset)}, device_id_type=MESH)

    load_codes = pltpu.make_async_copy(hc_hbm, hc, hc_sem)
    load_codes.start()
    load_ts = pltpu.make_async_copy(ts_hbm, ts_ref, ts_sem)
    load_ts.start()
    load_cs = pltpu.make_async_copy(cs_hbm, cs_ref, cs_sem)
    load_cs.start()
    rows = UNITS // 4
    load_w = [
        pltpu.make_async_copy(w_hbm.at[pl.ds(i * rows, rows)], w.at[pl.ds(i * rows, rows)], w_sem.at[i])
        for i in range(4)
    ]
    for copy in load_w:
        copy.start()
    load_r = pltpu.make_async_copy(r_hbm, r, r_sem)
    load_r.start()

    load_codes.wait()
    flipped = hc[...] ^ 0x888
    for k in range(4):
        codes[pl.ds(k * T, T), :WORDS] = nibble(flipped, k).astype(F32).astype(BF16)
        codes[pl.ds(k * T, T), WORDS:] = jnp.zeros((T, WIDE - WORDS), BF16)

    pl.semaphore_wait(barrier, len(PEERS))

    def rows_of(device):
        return pl.ds(pl.multiple_of(device * SLICE, SLICE), SLICE)

    gather = []
    for i, offset in enumerate(PEERS):
        target = at(*offset)
        gather.append(remote(codes.at[rows_of(target)], gathered.at[me], g_send.at[i], g_recv.at[i], target))
        gather[-1].start()
    gathered[me] = codes[rows_of(me), :]

    for i, copy in enumerate(load_w):
        copy.wait()

        def unpack(step, carry, i=i):
            at_rows = pl.ds(pl.multiple_of(i * rows + step * 32, 32), 32)
            for c in range(SIDE):
                block = w[at_rows, c * WIDE : (c + 1) * WIDE] ^ 0x888
                for k in range(4):
                    wbf[4 * k + c, at_rows, :] = nibble(block, k).astype(F32).astype(BF16)
            return carry

        lax.fori_loop(0, rows // 32, unpack, 0)
    row_id = lax.broadcasted_iota(jnp.int32, (T, T), 0)
    col_id = lax.broadcasted_iota(jnp.int32, (T, T), 1)
    load_ts.wait()
    scales = jnp.broadcast_to(ts_ref[...].reshape(1, T), (T, T))
    ts_col[...] = jnp.sum(jnp.where(row_id == col_id, scales, 0.0), axis=1, keepdims=True) * (
        1.0 / math.sqrt(FF)
    )

    for copy in gather:
        copy.wait_recv()
    for part in range(SLICE // 16):
        at_rows = pl.ds(part * 16, 16)
        for device, value in enumerate(hadamard([gathered[i, at_rows, :] for i in range(N_MP)])):
            mixed[device, at_rows, :] = value
    back = []
    for i, offset in enumerate(PEERS):
        target = at(*offset)
        back.append(remote(mixed.at[target], z.at[rows_of(me)], z_send.at[i], z_recv.at[i], target))
        back[-1].start()
    z[rows_of(me), :] = mixed[me]

    load_r.wait()
    for copy in back:
        copy.wait_recv()
    total = jnp.dot(z[pl.ds(0, T), :], r[0], preferred_element_type=F32)
    for k in range(1, 4):
        total += jnp.dot(z[pl.ds(k * T, T), :], r[k], preferred_element_type=F32)
    rot[...] = (total * ts_col[...]).astype(BF16)

    first_a, first_b = {}, {}
    for dy, dx in ORDER:
        product = jnp.dot(rot[...], wbf[at(dy, dx)], preferred_element_type=F32).astype(BF16)
        sa[dy, dx] = product[:, :HALF]
        sb[dx, dy] = product[:, HALF:]
        i = 4 * dy + dx
        if dx:
            first_a[dy, dx] = remote(sa.at[dy, dx], ra.at[dy, dx], a_send.at[i], a_recv.at[i], at(0, dx))
            first_a[dy, dx].start()
        if dy:
            first_b[dx, dy] = remote(sb.at[dx, dy], rb.at[dx, dy], b_send.at[i], b_recv.at[i], at(dy, 0))
            first_b[dx, dy].start()

    def summed(own, arrived, copies, major):
        total = own[major, 0].astype(F32)
        for minor in range(1, SIDE):
            copies[major, minor].wait_recv()
            total += arrived[major, minor].astype(F32)
        return total

    second_a, second_b = {}, {}
    for d in (2, 1, 3):
        ta[d] = summed(sa, ra, first_a, d).astype(BF16)
        second_a[d] = remote(ta.at[d], fa.at[d], ta_send.at[d], ta_recv.at[d], at(d, 0))
        second_a[d].start()
        tb[d] = summed(sb, rb, first_b, d).astype(BF16)
        second_b[d] = remote(tb.at[d], fb.at[d], tb_send.at[d], tb_recv.at[d], at(0, d))
        second_b[d].start()
    load_cs.wait()
    scale = cs_ref[...].reshape(1, WIDE)
    total_a = summed(sa, ra, first_a, 0)
    total_b = summed(sb, rb, first_b, 0)
    for d in (2, 1, 3):
        second_a[d].wait_recv()
        total_a += fa[d].astype(F32)
    out_ref[:, :HALF] = (total_a * scale[:, :HALF]).astype(BF16)
    for d in (2, 1, 3):
        second_b[d].wait_recv()
        total_b += fb[d].astype(F32)
    out_ref[:, HALF:] = (total_b * scale[:, HALF:]).astype(BF16)

    for copies in (gather, back, first_a.values(), first_b.values(), second_a.values(), second_b.values()):
        for copy in copies:
            copy.wait_send()


def on_device(hidden_codes, token_scales, weight_codes, column_scales):
    table = jnp.asarray(local_table(), BF16)
    dma = pltpu.SemaphoreType.DMA
    vmem = pl.BlockSpec(memory_space=pltpu.VMEM)
    hbm = pl.BlockSpec(memory_space=pltpu.HBM)
    sums = pltpu.VMEM((SIDE, SIDE, T, HALF), BF16)
    ends = pltpu.VMEM((SIDE, T, HALF), BF16)
    return pl.pallas_call(
        kernel,
        out_shape=jax.ShapeDtypeStruct((T, WIDE), BF16),
        in_specs=[hbm] * 5,
        out_specs=vmem,
        scratch_shapes=[
            pltpu.VMEM((T, WORDS), jnp.int32),
            pltpu.VMEM((T,), F32),
            pltpu.VMEM((UNITS, 4 * WIDE), jnp.int32),
            pltpu.VMEM((WIDE,), F32),
            pltpu.VMEM((4, WIDE, UNITS), BF16),
            pltpu.VMEM((4 * T, WIDE), BF16),
            pltpu.VMEM((N_MP, SLICE, WIDE), BF16),
            pltpu.VMEM((N_MP, SLICE, WIDE), BF16),
            pltpu.VMEM((4 * T, WIDE), BF16),
            pltpu.VMEM((T, UNITS), BF16),
            pltpu.VMEM((N_MP, UNITS, WIDE), BF16),
            pltpu.VMEM((T, 1), F32),
            sums, sums, sums, sums, ends, ends, ends, ends,
            dma, dma, dma((4,)), dma, dma,
            dma((15,)), dma((15,)), dma((15,)), dma((15,)),
            dma((16,)), dma((16,)), dma((16,)), dma((16,)),
            dma((4,)), dma((4,)), dma((4,)), dma((4,)),
        ],
        compiler_params=pltpu.CompilerParams(
            collective_id=0, has_side_effects=True, vmem_limit_bytes=64 * 2**20
        ),
    )(hidden_codes, token_scales, weight_codes, column_scales, table)


def solution(mesh):
    return jax.shard_map(
        on_device,
        mesh=mesh,
        in_specs=(P("dp", "mp"), P("dp"), P("mp", None), P("mp")),
        out_specs=P("dp", "mp"),
        check_vma=False,
    )
```

```python
import math

import jax
import jax.numpy as jnp
import numpy as np
from jax import lax
from jax.experimental import pallas as pl
from jax.experimental.pallas import tpu as pltpu
from jax.sharding import PartitionSpec as P

HC = 28
FF = 14336
SIDE = 4
N_MP = 16
T = 192
CHUNKS = ((0, 96), (96, 96))
WORDS = 224
WIDE = 256
UNITS = 896
HALF = 128
W_PARTS = 4
F32 = jnp.float32
BF16 = jnp.bfloat16
MESH = pl.DeviceIdType.MESH

HOPS = (0, 1, 2, 1)
PEERS = sorted(
    [(ey, ex) for ey in range(SIDE) for ex in range(SIDE) if ey or ex],
    key=lambda o: -(HOPS[o[0]] + HOPS[o[1]]),
)
ORDER = [
    ((1, 2), ""), ((3, 2), ""), ((2, 2), "a2"), ((2, 1), ""), ((2, 3), "b2"),
    ((1, 1), ""), ((3, 1), "a1"), ((1, 3), "b1"), ((3, 3), "a3 b3"),
    ((0, 1), ""), ((0, 2), ""), ((0, 3), ""), ((1, 0), ""), ((2, 0), ""), ((3, 0), ""), ((0, 0), ""),
]


def paley_table():
    modulus = 13
    residues = set((value * value % modulus for value in range(1, modulus)))
    symbols = np.array([0.0] + [1.0 if value in residues else -1.0 for value in range(1, modulus)])
    indices = np.arange(modulus)
    jacobsthal = symbols[(indices[None, :] - indices[:, None]) % modulus]
    first_row = np.concatenate([np.zeros((1, 1)), np.ones((1, modulus))], axis=1)
    other_rows = np.concatenate([np.ones((modulus, 1)), jacobsthal], axis=1)
    conference = np.concatenate([first_row, other_rows], axis=0)
    return np.kron(conference, np.array([[1.0, 1.0], [1.0, -1.0]])) + np.kron(
        np.eye(modulus + 1), np.array([[1.0, -1.0], [-1.0, -1.0]])
    )


def sylvester_table(length):
    indices = np.arange(length)
    intersection = indices[:, None] & indices[None, :]
    parity = intersection & 1
    for shift in range(1, max(length, 2).bit_length()):
        parity = parity ^ intersection >> shift & 1
    return 1.0 - 2.0 * parity


def local_table():
    table = np.kron(sylvester_table(UNITS // HC), paley_table())
    rows = 4 * np.arange(WORDS)[None, :] + np.arange(4)[:, None]
    out = np.zeros((4, WIDE, UNITS), np.float32)
    out[:, :WORDS] = table[rows]
    return out


def nibble(flipped, k):
    if k == 3:
        return flipped >> 12
    return (flipped << (28 - 4 * k)) >> 28


def hadamard(values):
    step = 1
    while step < len(values):
        values = [
            values[i ^ step] - values[i] if i & step else values[i] + values[i ^ step]
            for i in range(len(values))
        ]
        step *= 2
    return values


def other(place, e):
    if e == 1:
        return place + 1 - 2 * lax.rem(place, 2)
    if e == 2:
        return lax.rem(place + 2, SIDE)
    return 3 - place if e else place


class Sum:
    def __init__(self, remote, to_minor, to_major, buffers, sems):
        self.remote, self.to_minor, self.to_major = remote, to_minor, to_major
        self.s, self.r, self.keep, self.t, self.f = buffers
        self.sems = sems
        self.first, self.last = {}, {}

    def put(self, major, minor, value):
        if minor:
            self.s[minor, major] = value
        else:
            self.keep[major] = value

    def start_first(self, minor, group):
        majors, i = (pl.ds(1, 3), minor) if group == "far" else (pl.ds(0, 1), SIDE + minor)
        self.first[minor, group] = self.remote(
            self.s.at[minor, majors], self.r.at[minor, majors], self.sems[0].at[i], self.sems[1].at[i],
            self.to_minor(minor),
        )
        self.first[minor, group].start()

    def own(self, major):
        total = self.keep[major].astype(F32)
        for minor in range(1, SIDE):
            total += self.r[minor, major].astype(F32)
        return total

    def start_last(self):
        for minor in (1, 3, 2):
            self.first[minor, "far"].wait_recv()
        for major in (2, 1, 3):
            self.t[major] = self.own(major).astype(BF16)
            self.last[major] = self.remote(
                self.t.at[major], self.f.at[major], self.sems[2].at[major], self.sems[3].at[major], self.to_major(major)
            )
            self.last[major].start()

    def finish(self):
        for minor in (1, 3, 2):
            self.first[minor, "near"].wait_recv()
        total = self.own(0)
        for major in (1, 3, 2):
            self.last[major].wait_recv()
            total += self.f[major].astype(F32)
        return total

    def copies(self):
        return [*self.first.values(), *self.last.values()]


def kernel(*refs):
    (hc_hbm, ts_hbm, w_hbm, cs_hbm, r_hbm, out_ref), refs = refs[:6], refs[6:]
    (hc, ts_ref, w, cs_ref, r, wbf, ts_col), refs = refs[:7], refs[7:]
    (hc_sem, ts_sem, w_sem, cs_sem, r_sem), refs = refs[:5], refs[5:]
    chunks = [Chunk(start, size, refs[27 * c : 27 * (c + 1)]) for c, (start, size) in enumerate(CHUNKS)]

    me = lax.axis_index("mp")
    y, x = me // SIDE, me % SIDE

    def at(ey, ex):
        return other(y, ey) * SIDE + other(x, ex)

    def remote(src, dst, send, recv, target):
        return pltpu.make_async_remote_copy(
            src_ref=src, dst_ref=dst, send_sem=send, recv_sem=recv,
            device_id={"mp": target}, device_id_type=MESH,
        )

    load_codes = pltpu.make_async_copy(hc_hbm, hc, hc_sem)
    load_codes.start()
    barrier = pltpu.get_barrier_semaphore()
    for offset in PEERS:
        pl.semaphore_signal(barrier, inc=1, device_id={"mp": at(*offset)}, device_id_type=MESH)

    rows = UNITS // W_PARTS
    load_w = [
        pltpu.make_async_copy(w_hbm.at[pl.ds(i * rows, rows)], w.at[pl.ds(i * rows, rows)], w_sem.at[i])
        for i in range(W_PARTS)
    ]
    for copy in load_w:
        copy.start()
    load_ts = pltpu.make_async_copy(ts_hbm, ts_ref, ts_sem)
    load_cs = pltpu.make_async_copy(cs_hbm, cs_ref, cs_sem)
    load_r = pltpu.make_async_copy(r_hbm, r, r_sem)
    load_r.start()
    load_ts.start()
    load_cs.start()

    load_codes.wait()
    for c in chunks:
        flipped = hc[pl.ds(c.start, c.size), :] ^ 0x888
        for k in range(4):
            code = nibble(flipped, k).astype(F32).astype(BF16)
            c.codes[c.of(k), :] = code[:, :HALF]
            c.codes[c.of(4 + k), : WORDS - HALF] = code[:, HALF:]
            c.codes[c.of(4 + k), WORDS - HALF :] = jnp.zeros((c.size, WIDE - WORDS), BF16)

    pl.semaphore_wait(barrier, len(PEERS))

    for c in chunks:
        for i, offset in enumerate(PEERS):
            target = at(*offset)
            c.gather.append(
                remote(c.codes.at[c.slice(target)], c.gathered.at[me], c.g_send.at[i], c.g_recv.at[i], target)
            )
            c.gather[-1].start()
        c.gathered[me] = c.codes[c.slice(me), :]

    def unpack(i):
        load_w[i].wait()

        def some(step, carry):
            at_rows = pl.ds(pl.multiple_of(i * rows + step * 32, 32), 32)
            for column in range(SIDE):
                block = w[at_rows, column * WIDE : (column + 1) * WIDE] ^ 0x888
                for k in range(4):
                    wbf[4 * k + column, at_rows, :] = nibble(block, k).astype(F32).astype(BF16)
            return carry

        lax.fori_loop(0, rows // 32, some, 0)

    for i in range(W_PARTS // 2):
        unpack(i)

    for c in chunks:
        for copy in c.gather:
            copy.wait_recv()
        for part in range(c.rows // 16):
            at_rows = pl.ds(part * 16, 16)
            for device, value in enumerate(hadamard([c.gathered[i, at_rows, :] for i in range(N_MP)])):
                c.mixed[device, at_rows, :] = value
        for i, offset in enumerate(PEERS):
            target = at(*offset)
            c.back.append(remote(c.mixed.at[target], c.z.at[c.slice(me)], c.z_send.at[i], c.z_recv.at[i], target))
            c.back[-1].start()
        c.z[c.slice(me), :] = c.mixed[me]

    for i in range(W_PARTS // 2, W_PARTS):
        unpack(i)
    load_ts.wait()
    row_id = lax.broadcasted_iota(jnp.int32, (T, T), 0)
    col_id = lax.broadcasted_iota(jnp.int32, (T, T), 1)
    scales = jnp.broadcast_to(ts_ref[...].reshape(1, T), (T, T))
    ts_col[...] = jnp.sum(jnp.where(row_id == col_id, scales, 0.0), axis=1, keepdims=True) * (
        1.0 / math.sqrt(FF)
    )
    load_r.wait()
    load_cs.wait()

    for c in chunks:
        for copy in c.back:
            copy.wait_recv()
        total = jnp.zeros((c.size, UNITS), F32)
        for k in range(4):
            some = jnp.concatenate([c.z[c.of(k), :], c.z[c.of(4 + k), :]], axis=1)
            total += jnp.dot(some, r[k], preferred_element_type=F32)
        c.rot[...] = (total * ts_col[pl.ds(c.start, c.size), :]).astype(BF16)

        c.a = Sum(remote, lambda e: at(0, e), lambda e: at(e, 0), c.buffers_a, c.sems_a)
        c.b = Sum(remote, lambda e: at(e, 0), lambda e: at(0, e), c.buffers_b, c.sems_b)
        for (ey, ex), ready in ORDER:
            product = jnp.dot(c.rot[...], wbf[at(ey, ex)], preferred_element_type=F32).astype(BF16)
            c.a.put(ey, ex, product[:, :HALF])
            c.b.put(ex, ey, product[:, HALF:])
            for name in ready.split():
                getattr(c, name[0]).start_first(int(name[1]), "far")
        if c is not chunks[-1]:
            for minor in (2, 1, 3):
                c.a.start_first(minor, "near")
                c.b.start_first(minor, "near")

    for c in chunks:
        c.a.start_last()
        c.b.start_last()
        if c is chunks[-2]:
            for minor in (2, 1, 3):
                chunks[-1].a.start_first(minor, "near")
                chunks[-1].b.start_first(minor, "near")
    scale = cs_ref[...].reshape(1, WIDE)
    for c in chunks:
        out_ref[pl.ds(c.start, c.size), :HALF] = (c.a.finish() * scale[:, :HALF]).astype(BF16)
        out_ref[pl.ds(c.start, c.size), HALF:] = (c.b.finish() * scale[:, HALF:]).astype(BF16)

    for c in chunks:
        for copy in [*c.gather, *c.back, *c.a.copies(), *c.b.copies()]:
            copy.wait_send()


def chunk_scratch(size):
    dma = pltpu.SemaphoreType.DMA
    sliced = pltpu.VMEM((N_MP, size // 2, HALF), BF16)
    stacked = pltpu.VMEM((8 * size, HALF), BF16)
    blocks = pltpu.VMEM((SIDE, SIDE, size, HALF), BF16)
    row = pltpu.VMEM((SIDE, size, HALF), BF16)
    peers = dma((len(PEERS),))
    return [
        stacked, sliced, sliced, stacked, pltpu.VMEM((size, UNITS), BF16),
        *([blocks, blocks, row, row, row] * 2),
        *([peers] * 4),
        *([dma((2 * SIDE,)), dma((2 * SIDE,)), dma((SIDE,)), dma((SIDE,))] * 2),
    ]


class Chunk:
    def __init__(self, start, size, refs):
        self.start, self.size, self.rows = start, size, size // 2
        self.codes, self.gathered, self.mixed, self.z, self.rot = refs[:5]
        self.buffers_a, self.buffers_b = refs[5:10], refs[10:15]
        self.g_send, self.g_recv, self.z_send, self.z_recv = refs[15:19]
        self.sems_a, self.sems_b = refs[19:23], refs[23:27]
        self.gather, self.back = [], []

    def of(self, k):
        return pl.ds(k * self.size, self.size)

    def slice(self, device):
        return pl.ds(pl.multiple_of(device * self.rows, self.rows), self.rows)


def on_device(hidden_codes, token_scales, weight_codes, column_scales):
    operands = (hidden_codes, token_scales, weight_codes, column_scales, jnp.asarray(local_table(), BF16))
    dma = pltpu.SemaphoreType.DMA
    hbm = pl.BlockSpec(memory_space=pltpu.HBM)
    return pl.pallas_call(
        kernel,
        out_shape=jax.ShapeDtypeStruct((T, WIDE), BF16),
        in_specs=[hbm] * 5,
        out_specs=pl.BlockSpec(memory_space=pltpu.VMEM),
        scratch_shapes=[
            pltpu.VMEM((T, WORDS), jnp.int32),
            pltpu.VMEM((T,), F32),
            pltpu.VMEM((UNITS, 4 * WIDE), jnp.int32),
            pltpu.VMEM((WIDE,), F32),
            pltpu.VMEM((4, WIDE, UNITS), BF16),
            pltpu.VMEM((N_MP, UNITS, WIDE), BF16),
            pltpu.VMEM((T, 1), F32),
            dma, dma, dma((W_PARTS,)), dma, dma,
            *[ref for _, size in CHUNKS for ref in chunk_scratch(size)],
        ],
        compiler_params=pltpu.CompilerParams(
            collective_id=0, has_side_effects=True, vmem_limit_bytes=48 * 2**20
        ),
    )(*[pltpu.with_memory_space_constraint(operand, pltpu.HBM) for operand in operands])


def solution(mesh):
    return jax.shard_map(
        on_device,
        mesh=mesh,
        in_specs=(P("dp", "mp"), P("dp"), P("mp", None), P("mp")),
        out_specs=P("dp", "mp"),
        check_vma=False,
    )
```

```python
import math

import jax
import jax.numpy as jnp
import numpy as np
from jax import lax
from jax.experimental import pallas as pl
from jax.experimental.pallas import tpu as pltpu
from jax.sharding import PartitionSpec as P

HC = 28
FF = 14336
SIDE = 4
N_MP = 16
T = 192
CHUNKS = ((0, 96), (96, 96))
GATHER = ((0, 0), (0, 0))
NEAR = ((0, 0), (2, 2))
WORDS = 224
WIDE = 256
UNITS = 896
HALF = 128
W_PARTS = 4
F32 = jnp.float32
BF16 = jnp.bfloat16
MESH = pl.DeviceIdType.MESH

HOPS = (0, 1, 2, 1)
PEERS = sorted(
    [(ey, ex) for ey in range(SIDE) for ex in range(SIDE) if ey or ex],
    key=lambda o: -(HOPS[o[0]] + HOPS[o[1]]),
)
ORDER = [
    ((1, 2), ""), ((3, 2), ""), ((2, 2), "a2"), ((2, 1), ""), ((2, 3), "b2"),
    ((1, 1), ""), ((3, 1), "a1"), ((1, 3), "b1"), ((3, 3), "a3 b3"),
    ((0, 1), ""), ((0, 2), ""), ((0, 3), ""), ((1, 0), ""), ((2, 0), ""), ((3, 0), ""), ((0, 0), ""),
]


def paley_table():
    modulus = 13
    residues = set((value * value % modulus for value in range(1, modulus)))
    symbols = np.array([0.0] + [1.0 if value in residues else -1.0 for value in range(1, modulus)])
    indices = np.arange(modulus)
    jacobsthal = symbols[(indices[None, :] - indices[:, None]) % modulus]
    first_row = np.concatenate([np.zeros((1, 1)), np.ones((1, modulus))], axis=1)
    other_rows = np.concatenate([np.ones((modulus, 1)), jacobsthal], axis=1)
    conference = np.concatenate([first_row, other_rows], axis=0)
    return np.kron(conference, np.array([[1.0, 1.0], [1.0, -1.0]])) + np.kron(
        np.eye(modulus + 1), np.array([[1.0, -1.0], [-1.0, -1.0]])
    )


def sylvester_table(length):
    indices = np.arange(length)
    intersection = indices[:, None] & indices[None, :]
    parity = intersection & 1
    for shift in range(1, max(length, 2).bit_length()):
        parity = parity ^ intersection >> shift & 1
    return 1.0 - 2.0 * parity


def local_table():
    table = np.kron(sylvester_table(UNITS // HC), paley_table())
    rows = 4 * np.arange(WORDS)[None, :] + np.arange(4)[:, None]
    out = np.zeros((4, WIDE, UNITS), np.float32)
    out[:, :WORDS] = table[rows]
    return out


def nibble(flipped, k):
    if k == 3:
        return flipped >> 12
    return (flipped << (28 - 4 * k)) >> 28


def hadamard(values):
    step = 1
    while step < len(values):
        values = [
            values[i ^ step] - values[i] if i & step else values[i] + values[i ^ step]
            for i in range(len(values))
        ]
        step *= 2
    return values


def other(place, e):
    if e == 1:
        return place + 1 - 2 * lax.rem(place, 2)
    if e == 2:
        return lax.rem(place + 2, SIDE)
    return 3 - place if e else place


def wait_bytes(ref, sem):
    pltpu.make_async_copy(ref, ref, sem).wait()


class Sum:
    def __init__(self, remote, to_minor, to_major, buffers, sems):
        self.remote, self.to_minor, self.to_major = remote, to_minor, to_major
        self.s, self.r, self.keep, self.t, self.f = buffers
        self.first_send, self.far, self.near, self.last_send, self.last = (sems.at[i] for i in range(5))

    def put(self, major, minor, value):
        if minor:
            self.s[minor, major] = value
        else:
            self.keep[major] = value

    def make_first(self, minor, group):
        far = group == "far"
        majors = pl.ds(1, 3) if far else pl.ds(0, 1)
        return self.remote(
            self.s.at[minor, majors], self.r.at[minor, majors], self.first_send, self.far if far else self.near,
            self.to_minor(minor),
        )

    def own(self, major):
        total = self.keep[major].astype(F32)
        for minor in range(1, SIDE):
            total += self.r[minor, major].astype(F32)
        return total

    def start_last(self):
        wait_bytes(self.r.at[pl.ds(1, 3), pl.ds(1, 3)], self.far)
        for major in (2, 1, 3):
            self.t[major] = self.own(major).astype(BF16)
            self.remote(
                self.t.at[major], self.f.at[major], self.last_send, self.last, self.to_major(major)
            ).start()

    def finish(self):
        wait_bytes(self.r.at[pl.ds(1, 3), pl.ds(0, 1)], self.near)
        total = self.own(0)
        wait_bytes(self.f.at[pl.ds(1, 3)], self.last)
        for major in (1, 3, 2):
            total += self.f[major].astype(F32)
        return total

    def wait_first_sends(self):
        wait_bytes(self.s.at[pl.ds(1, 3)], self.first_send)

    def wait_last_sends(self):
        wait_bytes(self.t.at[pl.ds(1, 3)], self.last_send)


def kernel(*refs):
    (hc_hbm, ts_hbm, w_hbm, cs_hbm, r_hbm, out_ref), refs = refs[:6], refs[6:]
    (hc, ts_ref, w, cs_ref, r, wbf, ts_col), refs = refs[:7], refs[7:]
    (hc_sem, ts_sem, w_sem, cs_sem, r_sem), refs = refs[:5], refs[5:]
    chunks = [Chunk(start, size, refs[18 * c : 18 * (c + 1)]) for c, (start, size) in enumerate(CHUNKS)]

    me = lax.axis_index("mp")
    y, x = me // SIDE, me % SIDE

    def at(ey, ex):
        return other(y, ey) * SIDE + other(x, ex)

    def remote(src, dst, send, recv, target):
        return pltpu.make_async_remote_copy(
            src_ref=src, dst_ref=dst, send_sem=send, recv_sem=recv,
            device_id={"mp": target}, device_id_type=MESH,
        )

    load_codes = pltpu.make_async_copy(hc_hbm, hc, hc_sem)
    load_codes.start()
    barrier = pltpu.get_barrier_semaphore()
    for offset in PEERS:
        pl.semaphore_signal(barrier, inc=1, device_id={"mp": at(*offset)}, device_id_type=MESH)

    rows = UNITS // W_PARTS
    load_w = [
        pltpu.make_async_copy(w_hbm.at[pl.ds(i * rows, rows)], w.at[pl.ds(i * rows, rows)], w_sem.at[i])
        for i in range(W_PARTS)
    ]
    for copy in load_w:
        copy.start()
    load_ts = pltpu.make_async_copy(ts_hbm, ts_ref, ts_sem)
    load_cs = pltpu.make_async_copy(cs_hbm, cs_ref, cs_sem)
    load_r = pltpu.make_async_copy(r_hbm, r, r_sem)
    load_r.start()
    load_ts.start()
    load_cs.start()

    load_codes.wait()
    for c in chunks:
        flipped = hc[pl.ds(c.start, c.size), :] ^ 0x888
        for k in range(4):
            code = nibble(flipped, k).astype(F32).astype(BF16)
            c.codes[c.of(k), :] = code[:, :HALF]
            c.codes[c.of(4 + k), : WORDS - HALF] = code[:, HALF:]
            c.codes[c.of(4 + k), WORDS - HALF :] = jnp.zeros((c.size, WIDE - WORDS), BF16)

    pl.semaphore_wait(barrier, len(PEERS))

    core = lax.rem(lax.axis_index("dp"), 2)

    def start_at(point, points, copies):
        def start():
            for copy in copies:
                copy.start()

        if points == (point, point):
            start()
        elif point in points:
            pl.when(core == points.index(point))(start)

    def start_gather(point):
        for c, points in zip(chunks, GATHER):
            start_at(point, points, c.gather)

    for c in chunks:
        for offset in PEERS:
            target = at(*offset)
            c.gather.append(remote(c.codes.at[c.slice(target)], c.gathered.at[me], c.g_send, c.g_recv, target))
        c.gathered[me] = c.codes[c.slice(me), :]
    start_gather(0)

    def unpack(i):
        load_w[i].wait()

        def some(step, carry):
            at_rows = pl.ds(pl.multiple_of(i * rows + step * 32, 32), 32)
            for column in range(SIDE):
                block = w[at_rows, column * WIDE : (column + 1) * WIDE] ^ 0x888
                for k in range(4):
                    wbf[4 * k + column, at_rows, :] = nibble(block, k).astype(F32).astype(BF16)
            return carry

        lax.fori_loop(0, rows // 32, some, 0)

    for i in range(W_PARTS // 2):
        unpack(i)
        start_gather(i + 1)

    for c in chunks:
        wait_bytes(c.gathered.at[pl.ds(0, len(PEERS))], c.g_recv)
        for part in range(c.rows // 16):
            at_rows = pl.ds(part * 16, 16)
            for device, value in enumerate(hadamard([c.gathered[i, at_rows, :] for i in range(N_MP)])):
                c.mixed[device, at_rows, :] = value
        for offset in PEERS:
            target = at(*offset)
            remote(c.mixed.at[target], c.z.at[c.slice(me)], c.z_send, c.z_recv, target).start()
        c.z[c.slice(me), :] = c.mixed[me]

    for i in range(W_PARTS // 2, W_PARTS):
        unpack(i)
    load_ts.wait()
    row_id = lax.broadcasted_iota(jnp.int32, (T, T), 0)
    col_id = lax.broadcasted_iota(jnp.int32, (T, T), 1)
    scales = jnp.broadcast_to(ts_ref[...].reshape(1, T), (T, T))
    ts_col[...] = jnp.sum(jnp.where(row_id == col_id, scales, 0.0), axis=1, keepdims=True) * (
        1.0 / math.sqrt(FF)
    )
    load_r.wait()
    load_cs.wait()

    def start_near(point):
        for c, points in zip(chunks, NEAR):
            start_at(point, points, getattr(c, "near", ()))

    for c in chunks:
        wait_bytes(c.z.at[pl.ds(0, len(PEERS) * c.rows)], c.z_recv)
        total = jnp.zeros((c.size, UNITS), F32)
        for k in range(4):
            some = jnp.concatenate([c.z[c.of(k), :], c.z[c.of(4 + k), :]], axis=1)
            total += jnp.dot(some, r[k], preferred_element_type=F32)
        c.rot[...] = (total * ts_col[pl.ds(c.start, c.size), :]).astype(BF16)

        c.a = Sum(remote, lambda e: at(0, e), lambda e: at(e, 0), c.buffers_a, c.sems_a)
        c.b = Sum(remote, lambda e: at(e, 0), lambda e: at(0, e), c.buffers_b, c.sems_b)
        for (ey, ex), ready in ORDER:
            product = jnp.dot(c.rot[...], wbf[at(ey, ex)], preferred_element_type=F32).astype(BF16)
            c.a.put(ey, ex, product[:, :HALF])
            c.b.put(ex, ey, product[:, HALF:])
            for name in ready.split():
                getattr(c, name[0]).make_first(int(name[1]), "far").start()
        c.near = [half.make_first(minor, "near") for minor in (2, 1, 3) for half in (c.a, c.b)]
        start_near(chunks.index(c))

    for c in chunks:
        wait_bytes(c.gathered.at[pl.ds(0, len(PEERS))], c.g_send)
        wait_bytes(c.z.at[pl.ds(0, len(PEERS) * c.rows)], c.z_send)
    for c in chunks:
        c.a.start_last()
        c.b.start_last()
        start_near(len(chunks) + chunks.index(c))
    for c in chunks:
        c.a.wait_first_sends()
        c.b.wait_first_sends()
    scale = cs_ref[...].reshape(1, WIDE)
    for c in chunks:
        out_ref[pl.ds(c.start, c.size), :HALF] = (c.a.finish() * scale[:, :HALF]).astype(BF16)
        out_ref[pl.ds(c.start, c.size), HALF:] = (c.b.finish() * scale[:, HALF:]).astype(BF16)

    for c in chunks:
        c.a.wait_last_sends()
        c.b.wait_last_sends()


def chunk_scratch(size):
    dma = pltpu.SemaphoreType.DMA
    sliced = pltpu.VMEM((N_MP, size // 2, HALF), BF16)
    stacked = pltpu.VMEM((8 * size, HALF), BF16)
    blocks = pltpu.VMEM((SIDE, SIDE, size, HALF), BF16)
    row = pltpu.VMEM((SIDE, size, HALF), BF16)
    return [
        stacked, sliced, sliced, stacked, pltpu.VMEM((size, UNITS), BF16),
        *([blocks, blocks, row, row, row] * 2),
        dma((4,)), dma((5,)), dma((5,)),
    ]


class Chunk:
    def __init__(self, start, size, refs):
        self.start, self.size, self.rows = start, size, size // 2
        self.codes, self.gathered, self.mixed, self.z, self.rot = refs[:5]
        self.buffers_a, self.buffers_b = refs[5:10], refs[10:15]
        self.g_send, self.g_recv, self.z_send, self.z_recv = (refs[15].at[i] for i in range(4))
        self.sems_a, self.sems_b = refs[16:18]
        self.gather = []

    def of(self, k):
        return pl.ds(k * self.size, self.size)

    def slice(self, device):
        return pl.ds(pl.multiple_of(device * self.rows, self.rows), self.rows)


def on_device(hidden_codes, token_scales, weight_codes, column_scales):
    operands = (hidden_codes, token_scales, weight_codes, column_scales, jnp.asarray(local_table(), BF16))
    dma = pltpu.SemaphoreType.DMA
    hbm = pl.BlockSpec(memory_space=pltpu.HBM)
    return pl.pallas_call(
        kernel,
        out_shape=jax.ShapeDtypeStruct((T, WIDE), BF16),
        in_specs=[hbm] * 5,
        out_specs=pl.BlockSpec(memory_space=pltpu.VMEM),
        scratch_shapes=[
            pltpu.VMEM((T, WORDS), jnp.int32),
            pltpu.VMEM((T,), F32),
            pltpu.VMEM((UNITS, 4 * WIDE), jnp.int32),
            pltpu.VMEM((WIDE,), F32),
            pltpu.VMEM((4, WIDE, UNITS), BF16),
            pltpu.VMEM((N_MP, UNITS, WIDE), BF16),
            pltpu.VMEM((T, 1), F32),
            dma, dma, dma((W_PARTS,)), dma, dma,
            *[ref for _, size in CHUNKS for ref in chunk_scratch(size)],
        ],
        compiler_params=pltpu.CompilerParams(
            collective_id=0, has_side_effects=True, vmem_limit_bytes=48 * 2**20
        ),
    )(*[pltpu.with_memory_space_constraint(operand, pltpu.HBM) for operand in operands])


def solution(mesh):
    return jax.shard_map(
        on_device,
        mesh=mesh,
        in_specs=(P("dp", "mp"), P("dp"), P("mp", None), P("mp")),
        out_specs=P("dp", "mp"),
        check_vma=False,
    )
```

```python
import math

import jax
import jax.numpy as jnp
import numpy as np
from jax import lax
from jax.experimental import pallas as pl
from jax.experimental.pallas import tpu as pltpu
from jax.sharding import PartitionSpec as P

HC = 28
FF = 14336
SIDE = 4
N_MP = 16
T = 192
CHUNKS = ((0, 96), (96, 96))
GATHER = ((0, 0), (0, 0))
NEAR = ((0, 0), (2, 2))
WORDS = 224
WIDE = 256
UNITS = 896
HALF = 128
W_PARTS = 4
F32 = jnp.float32
BF16 = jnp.bfloat16
MESH = pl.DeviceIdType.MESH

HOPS = (0, 1, 2, 1)
PEERS = sorted(
    [(ey, ex) for ey in range(SIDE) for ex in range(SIDE) if ey or ex],
    key=lambda o: -(HOPS[o[0]] + HOPS[o[1]]),
)
ORDER = [
    (2, 2), (1, 2), (2, 1), (3, 2), (2, 3), (1, 1), (3, 1), (1, 3), (3, 3),
    (0, 1), (0, 2), (0, 3), (1, 0), (2, 0), (3, 0), (0, 0),
]


def paley_table():
    modulus = 13
    residues = set((value * value % modulus for value in range(1, modulus)))
    symbols = np.array([0.0] + [1.0 if value in residues else -1.0 for value in range(1, modulus)])
    indices = np.arange(modulus)
    jacobsthal = symbols[(indices[None, :] - indices[:, None]) % modulus]
    first_row = np.concatenate([np.zeros((1, 1)), np.ones((1, modulus))], axis=1)
    other_rows = np.concatenate([np.ones((modulus, 1)), jacobsthal], axis=1)
    conference = np.concatenate([first_row, other_rows], axis=0)
    return np.kron(conference, np.array([[1.0, 1.0], [1.0, -1.0]])) + np.kron(
        np.eye(modulus + 1), np.array([[1.0, -1.0], [-1.0, -1.0]])
    )


def sylvester_table(length):
    indices = np.arange(length)
    intersection = indices[:, None] & indices[None, :]
    parity = intersection & 1
    for shift in range(1, max(length, 2).bit_length()):
        parity = parity ^ intersection >> shift & 1
    return 1.0 - 2.0 * parity


def local_table():
    table = np.kron(sylvester_table(UNITS // HC), paley_table())
    rows = 4 * np.arange(WORDS)[None, :] + np.arange(4)[:, None]
    out = np.zeros((4, WIDE, UNITS), np.float32)
    out[:, :WORDS] = table[rows]
    return out


def nibble(flipped, k):
    if k == 3:
        return flipped >> 12
    return (flipped << (28 - 4 * k)) >> 28


def hadamard(values):
    step = 1
    while step < len(values):
        values = [
            values[i ^ step] - values[i] if i & step else values[i] + values[i ^ step]
            for i in range(len(values))
        ]
        step *= 2
    return values


def other(place, e):
    if e == 1:
        return place + 1 - 2 * lax.rem(place, 2)
    if e == 2:
        return lax.rem(place + 2, SIDE)
    return 3 - place if e else place


def wait_bytes(ref, sem):
    pltpu.make_async_copy(ref, ref, sem).wait()


class Sum:
    def __init__(self, remote, to_minor, to_major, buffers, sems):
        self.remote, self.to_minor, self.to_major = remote, to_minor, to_major
        self.s, self.r, self.keep, self.t, self.f = buffers
        self.first_send, self.far, self.near, self.last_send, self.last = (sems.at[i] for i in range(5))

    def put(self, major, minor, value):
        if minor:
            self.s[minor, major] = value
        else:
            self.keep[major] = value

    def make_first(self, minor, major):
        far = major > 0
        majors = pl.ds(major, 1)
        return self.remote(
            self.s.at[minor, majors], self.r.at[minor, majors], self.first_send, self.far if far else self.near,
            self.to_minor(minor),
        )

    def own(self, major):
        total = self.keep[major].astype(F32)
        for minor in range(1, SIDE):
            total += self.r[minor, major].astype(F32)
        return total

    def start_last(self):
        wait_bytes(self.r.at[pl.ds(1, 3), pl.ds(1, 3)], self.far)
        for major in (2, 1, 3):
            self.t[major] = self.own(major).astype(BF16)
            self.remote(
                self.t.at[major], self.f.at[major], self.last_send, self.last, self.to_major(major)
            ).start()

    def finish(self):
        wait_bytes(self.r.at[pl.ds(1, 3), pl.ds(0, 1)], self.near)
        total = self.own(0)
        wait_bytes(self.f.at[pl.ds(1, 3)], self.last)
        for major in (1, 3, 2):
            total += self.f[major].astype(F32)
        return total

    def wait_first_sends(self):
        wait_bytes(self.s.at[pl.ds(1, 3)], self.first_send)

    def wait_last_sends(self):
        wait_bytes(self.t.at[pl.ds(1, 3)], self.last_send)


def kernel(*refs):
    (hc_hbm, ts_hbm, w_hbm, cs_hbm, r_hbm, out_ref), refs = refs[:6], refs[6:]
    (hc, ts_ref, w, cs_ref, r, wbf, ts_col), refs = refs[:7], refs[7:]
    (hc_sem, ts_sem, w_sem, cs_sem, r_sem), refs = refs[:5], refs[5:]
    chunks = [Chunk(start, size, refs[18 * c : 18 * (c + 1)]) for c, (start, size) in enumerate(CHUNKS)]

    me = lax.axis_index("mp")
    y, x = me // SIDE, me % SIDE

    def at(ey, ex):
        return other(y, ey) * SIDE + other(x, ex)

    def remote(src, dst, send, recv, target):
        return pltpu.make_async_remote_copy(
            src_ref=src, dst_ref=dst, send_sem=send, recv_sem=recv,
            device_id={"mp": target}, device_id_type=MESH,
        )

    load_codes = pltpu.make_async_copy(hc_hbm, hc, hc_sem)
    load_codes.start()
    barrier = pltpu.get_barrier_semaphore()
    for offset in PEERS:
        pl.semaphore_signal(barrier, inc=1, device_id={"mp": at(*offset)}, device_id_type=MESH)

    rows = UNITS // W_PARTS
    load_w = [
        pltpu.make_async_copy(w_hbm.at[pl.ds(i * rows, rows)], w.at[pl.ds(i * rows, rows)], w_sem.at[i])
        for i in range(W_PARTS)
    ]
    for copy in load_w:
        copy.start()
    load_ts = pltpu.make_async_copy(ts_hbm, ts_ref, ts_sem)
    load_cs = pltpu.make_async_copy(cs_hbm, cs_ref, cs_sem)
    load_r = pltpu.make_async_copy(r_hbm, r, r_sem)
    load_r.start()
    load_ts.start()
    load_cs.start()

    load_codes.wait()
    for c in chunks:
        flipped = hc[pl.ds(c.start, c.size), :] ^ 0x888
        for k in range(4):
            code = nibble(flipped, k).astype(F32).astype(BF16)
            c.codes[c.of(k), :] = code[:, :HALF]
            c.codes[c.of(4 + k), : WORDS - HALF] = code[:, HALF:]
            c.codes[c.of(4 + k), WORDS - HALF :] = jnp.zeros((c.size, WIDE - WORDS), BF16)

    pl.semaphore_wait(barrier, len(PEERS))

    core = lax.rem(lax.axis_index("dp"), 2)

    def start_at(point, points, copies):
        def start():
            for copy in copies:
                copy.start()

        if points == (point, point):
            start()
        elif point in points:
            pl.when(core == points.index(point))(start)

    def start_gather(point):
        for c, points in zip(chunks, GATHER):
            start_at(point, points, c.gather)

    for c in chunks:
        for offset in PEERS:
            target = at(*offset)
            c.gather.append(remote(c.codes.at[c.slice(target)], c.gathered.at[me], c.g_send, c.g_recv, target))
        c.gathered[me] = c.codes[c.slice(me), :]
    start_gather(0)

    def unpack(i):
        load_w[i].wait()

        def some(step, carry):
            at_rows = pl.ds(pl.multiple_of(i * rows + step * 32, 32), 32)
            for column in range(SIDE):
                block = w[at_rows, column * WIDE : (column + 1) * WIDE] ^ 0x888
                for k in range(4):
                    wbf[4 * k + column, at_rows, :] = nibble(block, k).astype(F32).astype(BF16)
            return carry

        lax.fori_loop(0, rows // 32, some, 0)

    for i in range(W_PARTS // 2):
        unpack(i)
        start_gather(i + 1)

    for c in chunks:
        wait_bytes(c.gathered.at[pl.ds(0, len(PEERS))], c.g_recv)
        for part in range(c.rows // 16):
            at_rows = pl.ds(part * 16, 16)
            for device, value in enumerate(hadamard([c.gathered[i, at_rows, :] for i in range(N_MP)])):
                c.mixed[device, at_rows, :] = value
        for offset in PEERS:
            target = at(*offset)
            remote(c.mixed.at[target], c.z.at[c.slice(me)], c.z_send, c.z_recv, target).start()
        c.z[c.slice(me), :] = c.mixed[me]

    for i in range(W_PARTS // 2, W_PARTS):
        unpack(i)
    load_ts.wait()
    row_id = lax.broadcasted_iota(jnp.int32, (T, T), 0)
    col_id = lax.broadcasted_iota(jnp.int32, (T, T), 1)
    scales = jnp.broadcast_to(ts_ref[...].reshape(1, T), (T, T))
    ts_col[...] = jnp.sum(jnp.where(row_id == col_id, scales, 0.0), axis=1, keepdims=True) * (
        1.0 / math.sqrt(FF)
    )
    load_r.wait()
    load_cs.wait()

    def start_near(point):
        for c, points in zip(chunks, NEAR):
            start_at(point, points, getattr(c, "near", ()))

    for c in chunks:
        wait_bytes(c.z.at[pl.ds(0, len(PEERS) * c.rows)], c.z_recv)
        total = jnp.zeros((c.size, UNITS), F32)
        for k in range(4):
            some = jnp.concatenate([c.z[c.of(k), :], c.z[c.of(4 + k), :]], axis=1)
            total += jnp.dot(some, r[k], preferred_element_type=F32)
        c.rot[...] = (total * ts_col[pl.ds(c.start, c.size), :]).astype(BF16)

        c.a = Sum(remote, lambda e: at(0, e), lambda e: at(e, 0), c.buffers_a, c.sems_a)
        c.b = Sum(remote, lambda e: at(e, 0), lambda e: at(0, e), c.buffers_b, c.sems_b)
        for ey, ex in ORDER:
            product = jnp.dot(c.rot[...], wbf[at(ey, ex)], preferred_element_type=F32).astype(BF16)
            c.a.put(ey, ex, product[:, :HALF])
            c.b.put(ex, ey, product[:, HALF:])
            if ey and ex:
                c.a.make_first(ex, ey).start()
                c.b.make_first(ey, ex).start()
        c.near = [half.make_first(minor, 0) for minor in (2, 1, 3) for half in (c.a, c.b)]
        start_near(chunks.index(c))

    for c in chunks:
        wait_bytes(c.gathered.at[pl.ds(0, len(PEERS))], c.g_send)
        wait_bytes(c.z.at[pl.ds(0, len(PEERS) * c.rows)], c.z_send)
    for c in chunks:
        c.a.start_last()
        c.b.start_last()
        start_near(len(chunks) + chunks.index(c))
    for c in chunks:
        c.a.wait_first_sends()
        c.b.wait_first_sends()
    scale = cs_ref[...].reshape(1, WIDE)
    for c in chunks:
        out_ref[pl.ds(c.start, c.size), :HALF] = (c.a.finish() * scale[:, :HALF]).astype(BF16)
        out_ref[pl.ds(c.start, c.size), HALF:] = (c.b.finish() * scale[:, HALF:]).astype(BF16)

    for c in chunks:
        c.a.wait_last_sends()
        c.b.wait_last_sends()


def chunk_scratch(size):
    dma = pltpu.SemaphoreType.DMA
    sliced = pltpu.VMEM((N_MP, size // 2, HALF), BF16)
    stacked = pltpu.VMEM((8 * size, HALF), BF16)
    blocks = pltpu.VMEM((SIDE, SIDE, size, HALF), BF16)
    row = pltpu.VMEM((SIDE, size, HALF), BF16)
    return [
        stacked, sliced, sliced, stacked, pltpu.VMEM((size, UNITS), BF16),
        *([blocks, blocks, row, row, row] * 2),
        dma((4,)), dma((5,)), dma((5,)),
    ]


class Chunk:
    def __init__(self, start, size, refs):
        self.start, self.size, self.rows = start, size, size // 2
        self.codes, self.gathered, self.mixed, self.z, self.rot = refs[:5]
        self.buffers_a, self.buffers_b = refs[5:10], refs[10:15]
        self.g_send, self.g_recv, self.z_send, self.z_recv = (refs[15].at[i] for i in range(4))
        self.sems_a, self.sems_b = refs[16:18]
        self.gather = []

    def of(self, k):
        return pl.ds(k * self.size, self.size)

    def slice(self, device):
        return pl.ds(pl.multiple_of(device * self.rows, self.rows), self.rows)


def on_device(hidden_codes, token_scales, weight_codes, column_scales):
    operands = (hidden_codes, token_scales, weight_codes, column_scales, jnp.asarray(local_table(), BF16))
    dma = pltpu.SemaphoreType.DMA
    hbm = pl.BlockSpec(memory_space=pltpu.HBM)
    return pl.pallas_call(
        kernel,
        out_shape=jax.ShapeDtypeStruct((T, WIDE), BF16),
        in_specs=[hbm] * 5,
        out_specs=pl.BlockSpec(memory_space=pltpu.VMEM),
        scratch_shapes=[
            pltpu.VMEM((T, WORDS), jnp.int32),
            pltpu.VMEM((T,), F32),
            pltpu.VMEM((UNITS, 4 * WIDE), jnp.int32),
            pltpu.VMEM((WIDE,), F32),
            pltpu.VMEM((4, WIDE, UNITS), BF16),
            pltpu.VMEM((N_MP, UNITS, WIDE), BF16),
            pltpu.VMEM((T, 1), F32),
            dma, dma, dma((W_PARTS,)), dma, dma,
            *[ref for _, size in CHUNKS for ref in chunk_scratch(size)],
        ],
        compiler_params=pltpu.CompilerParams(
            collective_id=0, has_side_effects=True, vmem_limit_bytes=48 * 2**20
        ),
    )(*[pltpu.with_memory_space_constraint(operand, pltpu.HBM) for operand in operands])


def solution(mesh):
    return jax.shard_map(
        on_device,
        mesh=mesh,
        in_specs=(P("dp", "mp"), P("dp"), P("mp", None), P("mp")),
        out_specs=P("dp", "mp"),
        check_vma=False,
    )
```
